128 devices in a mesh: tm: 16 (over z, x_lo, core), lat: 8 (over x_hi, y).
Axes of the slice: x: 4 (x_hi: 2, x_lo: 2; x = x_hi * 2 + x_lo), y: 4, z: 4, core: 2. Of those that a mesh axis runs over, the one named last changes fastest.
Arguments:
- field: bfloat16 [2560, 192, 360], P('tm', 'lat'), may hold values from -6 to 6
- time_factor: bfloat16 [2560, 2560], replicated, may hold values from -2 to 2
- lat_factor: bfloat16 [192, 192], replicated, may hold values from -2 to 2
- lon_factor: bfloat16 [360, 360], replicated, may hold values from -2 to 2
Outputs:
- weights: bfloat16 [2560, 69120], P(None, ('tm', 'lat'))
The draws below stay inside these ranges and needn't reach their ends.
All inputs are finite; a program needn't handle non-finite values.
Results may differ from the reference program's by a relative error of at most 0.0057.
Values may be sent and summed in bfloat16 or wider, within the bound.
No kernel may reach another device: no remote copies, remote signals or barrier semaphores. Data moves between devices by JAX's collectives and lax.ppermute only.
A program may use at most 64 MiB of HBM per device.

```python
import jax
import jax.numpy as jnp

LAT = 192
LON = 360
TIME = 2560


def symmetric_factor(noise, order):
    return jnp.eye(order, dtype=jnp.float32) + 0.25 * (noise + noise.T) / jnp.sqrt(jnp.float32(order))


def rough_noise(key, order):
    return jax.random.normal(key, (order, order), jnp.float32)


def draw_time_factor(key, part):
    key = jax.random.fold_in(key, 5)
    return symmetric_factor(rough_noise(key, TIME), TIME).astype(jnp.bfloat16)


def draw_lat_factor(key, part):
    key = jax.random.fold_in(key, 11)
    return symmetric_factor(rough_noise(key, LAT), LAT).astype(jnp.bfloat16)


def draw_lon_factor(key, part):
    key = jax.random.fold_in(key, 17)
    return symmetric_factor(rough_noise(key, LON), LON).astype(jnp.bfloat16)


def levels(rng, extent, cuts, smallest, largest):
    def one(position, parts):
        draws = jax.random.uniform(jax.random.fold_in(jax.random.fold_in(rng, 6), position), (parts,), jnp.float32, smallest / len(cuts), largest / len(cuts))
        return jnp.repeat(jnp.exp(draws), extent[position] // parts).reshape((-1,) + (1,) * (len(extent) - position - 1))

    loudness = one(*cuts[0])
    for cut in cuts[1:]:
        loudness = loudness * one(*cut)
    return loudness


def scatter_about(key, dims, deviation, limit, split=(), kind=jnp.bfloat16):
    result = jax.random.normal(key, dims, jnp.float32) * deviation
    if len(split) > 0:
        result = levels(key, dims, split, -0.22, 0.18) * result
    return jnp.clip(result, min=-limit, max=limit).astype(kind)


def setup_inputs(seed: int = 0) -> dict:
    splits = jax.random.split(jax.random.key(seed), 5)
    field = scatter_about(splits[0], (TIME, LAT, LON), 1.0, 6.0, ((0, 16), (1, 8)))
    time_factor = draw_time_factor(jax.random.fold_in(splits[4], 71), 0)
    lat_factor = draw_lat_factor(jax.random.fold_in(splits[4], 71), 0)
    lon_factor = draw_lon_factor(jax.random.fold_in(splits[4], 71), 0)
    return {"field": field, "time_factor": time_factor, "lat_factor": lat_factor, "lon_factor": lon_factor}


def reference(field, time_factor, lat_factor, lon_factor):
    flat = field.astype(jnp.float32).reshape(TIME * LAT, LON)
    first = jnp.dot(flat, lon_factor.astype(jnp.float32)).astype(jnp.bfloat16)
    first = first.reshape(TIME, LAT, LON)
    second = jnp.einsum("im,tmj->tij", lat_factor.astype(jnp.float32), first.astype(jnp.float32))
    second = second.astype(jnp.bfloat16).reshape(TIME, LAT * LON)
    weights = jnp.dot(time_factor.astype(jnp.float32), second.astype(jnp.float32))
    return weights.astype(jnp.bfloat16)
```

```python
import functools

import jax
import jax.numpy as jnp
from jax import lax
from jax.experimental import pallas as pl
from jax.experimental.pallas import tpu as pltpu
from jax.sharding import PartitionSpec as P

LANES = 128
CELLS = 540
BLOCK = 88
VMEM = 60 * 1024 * 1024


def mix_kernel(x_ref, lon_ref, lat_ref, out_ref, first_ref, second_ref):
    parts, hours, few, columns = x_ref.shape
    rows = parts * few
    third = rows // 3
    lon = lon_ref[...]
    for part in range(parts):
        x = x_ref[part].astype(jnp.float32).reshape(hours * few, columns).astype(jnp.bfloat16)
        first = jnp.dot(x, lon, preferred_element_type=jnp.float32)
        first_ref[part] = first.astype(jnp.bfloat16).astype(jnp.float32).reshape(hours, few, columns)
    lat = lat_ref[...]

    def hour(t, carry):
        f = first_ref[:, t].reshape(rows, columns).astype(jnp.bfloat16)
        s = jnp.dot(lat, f, preferred_element_type=jnp.float32)
        for k in range(3):
            width = min(LANES, columns - LANES * k)
            second_ref[k, pl.ds(t * rows, rows), :width] = s[:, LANES * k : LANES * k + width]
        return carry

    lax.fori_loop(0, hours, hour, 0)
    lane = lax.broadcasted_iota(jnp.int32, (24, LANES), 1)
    low = lax.broadcasted_iota(jnp.int32, (8, LANES), 0) < 4
    narrow = lane[:8] < 32

    def tile(v, k):
        return v[:, LANES * k : LANES * (k + 1)]

    def pack(tiles):
        body = [t[:16] for t in tiles[:4]]
        tails = [t[16:24] for t in tiles[:4]]
        for k in (0, 2):
            body.append(jnp.where(low, tails[k], pltpu.roll(tails[k + 1], 4, 0)))
        rest = tiles[4]
        last = jnp.where(
            narrow,
            rest[:8],
            jnp.where(lane[:8] < 64, pltpu.roll(rest[8:16], 32, 1), pltpu.roll(rest[16:24], 64, 1)),
        )
        body.append(last)
        return jnp.concatenate(body, axis=0).astype(jnp.bfloat16)

    def triple(p, carry):
        a, b, c = (
            jnp.concatenate([second_ref[jnp.int32(k), pl.ds(jnp.int32(r * third) + p, 24, rows), :] for k in range(3)], axis=1)
            for r in range(3)
        )
        b_up = pltpu.roll(b, 104, 1)
        out_ref[2 * p] = pack(
            [
                tile(a, 0),
                tile(a, 1),
                jnp.where(lane < 104, tile(a, 2), tile(b_up, 0)),
                tile(b_up, 1),
                tile(b_up, 2),
            ]
        )
        b_down = pltpu.roll(b, 204, 1)
        c_up = pltpu.roll(c, 180, 1)
        out_ref[2 * p + 1] = pack(
            [
                tile(b_down, 0),
                jnp.where(lane < 52, tile(b_down, 1), tile(c_up, 1)),
                tile(c_up, 2),
                tile(c_up, 0),
                tile(c_up, 1),
            ]
        )
        return carry

    lax.fori_loop(0, third, triple, 0)


def mix(x, lon, lat):
    parts, hours, few, columns = x.shape
    rows = parts * few
    return pl.pallas_call(
        mix_kernel,
        out_shape=jax.ShapeDtypeStruct((2 * rows // 3, BLOCK, LANES), jnp.bfloat16),
        scratch_shapes=[
            pltpu.VMEM((parts, hours, few, columns), jnp.float32),
            pltpu.VMEM((3, 24 * rows, LANES), jnp.float32),
        ],
        compiler_params=pltpu.CompilerParams(vmem_limit_bytes=VMEM),
    )(x, lon, lat)


def time_kernel(r_ref, t_ref, out_ref, g_ref, gt_ref):
    sources = r_ref.shape[0]
    total = gt_ref.shape[1]

    @pl.when(pl.program_id(0) == 0)
    def _():
        low = lax.broadcasted_iota(jnp.int32, (8, LANES), 0) < 4

        def pieces(r, k):
            if k == 4:
                last = r[80:88]
                return last, pltpu.roll(last, 96, 1), pltpu.roll(last, 64, 1), False
            tail = 64 + 8 * (k // 2)
            return r[16 * k : 16 * k + 8], r[16 * k + 8 : 16 * k + 16], r[tail : tail + 8], k % 2 == 1

        def unpack(pair, carry):
            r0 = r_ref[2 * pair].astype(jnp.float32)
            r1 = r_ref[2 * pair + 1].astype(jnp.float32)
            start = pl.multiple_of(pair * 40, 8)
            for k in range(5):
                a0, a1, a2, high = pieces(r0, k)
                b0, b1, b2, _ = pieces(r1, k)
                if high:
                    a2 = pltpu.roll(a2, 4, 0)
                else:
                    b2 = pltpu.roll(b2, 4, 0)
                b0, b1 = pltpu.roll(b0, 4, 0), pltpu.roll(b1, 4, 0)
                both = [a0, a1, jnp.where(low, a2, b0), jnp.where(low, b0, b1), jnp.where(low, b1, b2)]
                g_ref[pl.ds(start, 40), LANES * k : LANES * (k + 1)] = jnp.concatenate(both, axis=0)
            return carry

        lax.fori_loop(0, sources // 2, unpack, 0)
        for k in range(5):
            width = min(LANES, gt_ref.shape[0] - LANES * k)
            for h in range(0, total, 512):
                block = g_ref[h : h + 512, LANES * k : LANES * (k + 1)]
                gt_ref[LANES * k : LANES * k + width, h : h + 512] = block.T[:width].astype(jnp.bfloat16)

    w = lax.dot_general(
        gt_ref[...], t_ref[...], (((1,), (1,)), ((), ())), preferred_element_type=jnp.float32
    )
    out_ref[...] = w[:CELLS].astype(jnp.bfloat16)


def time_product(r, time_factor):
    few = 256
    total = time_factor.shape[1]
    return pl.pallas_call(
        time_kernel,
        grid=(time_factor.shape[0] // few,),
        in_specs=[
            pl.BlockSpec(r.shape, lambda i: (0, 0, 0)),
            pl.BlockSpec((few, total), lambda i: (i, 0)),
        ],
        out_specs=pl.BlockSpec((CELLS, few), lambda i: (0, i)),
        out_shape=jax.ShapeDtypeStruct((CELLS, time_factor.shape[0]), jnp.bfloat16),
        scratch_shapes=[
            pltpu.VMEM((total, 5 * LANES), jnp.float32),
            pltpu.VMEM((544, total), jnp.bfloat16),
        ],
        compiler_params=pltpu.CompilerParams(vmem_limit_bytes=VMEM),
    )(r, time_factor)


def on_device(field, time_factor, lat_factor, lon_factor):
    hours, few, columns = field.shape
    parts = lax.axis_size("lat")
    moved = lax.all_to_all(field, "lat", split_axis=0, concat_axis=0, tiled=True)
    moved = moved.reshape(parts, hours // parts, few, columns)
    rows = lat_factor.shape[0]
    lat = lat_factor.reshape(rows // 3, 3, rows).transpose(1, 0, 2).reshape(rows, rows)
    blocks = mix(moved, lon_factor, lat)
    gathered = lax.all_to_all(blocks, ("tm", "lat"), split_axis=0, concat_axis=0, tiled=True)
    return time_product(gathered, time_factor).T


def solution(mesh):
    return jax.shard_map(
        on_device,
        mesh=mesh,
        in_specs=(P("tm", "lat", None), P(), P(), P()),
        out_specs=P(None, ("tm", "lat")),
        check_vma=False,
    )
```

```python
import jax
import jax.numpy as jnp
from jax import lax
from jax.experimental import pallas as pl
from jax.experimental.pallas import tpu as pltpu
from jax.sharding import PartitionSpec as P

LANES = 128
CELLS = 540
TALL = 544
HOURS = 20
MAIN = 16
BLOCK = 88
GROUP = 32 * HOURS
STRIDE = 200
COPIES = 8
WHOLE = pl.BlockSpec(memory_space=pltpu.VMEM)
OUTSIDE = pl.BlockSpec(memory_space=pltpu.HBM)


def params(mib):
    return pltpu.CompilerParams(vmem_limit_bytes=mib * 1024 * 1024)


def tile(v, k):
    return v[:, LANES * k : LANES * (k + 1)]


def pack(tiles, row, lane):
    tails = [jnp.where(row < 4, tiles[k][16:], pltpu.roll(tiles[k + 1][16:], 4, 0)) for k in (0, 2)]
    rest = tiles[4]
    last = jnp.where(
        lane < 32,
        rest[:8],
        jnp.where(lane < 64, pltpu.roll(rest[8:16], 32, 1), pltpu.roll(rest[16:], 64, 1)),
    )
    return jnp.concatenate([t[:16] for t in tiles[:4]] + tails + [last], axis=0).astype(jnp.bfloat16)


def mix_kernel(x_ref, lon_ref, lat_ref, to_ref, first_ref, second_ref, out_ref, sem):
    parts, hours, few, columns = x_ref.shape
    rows = parts * few
    third = rows // 3
    lon = lon_ref[...]

    def part_of_first(part, carry):
        x = x_ref[part].astype(jnp.float32).reshape(hours * few, columns).astype(jnp.bfloat16)
        first = jnp.dot(x, lon, preferred_element_type=jnp.float32)
        first_ref[part] = first.reshape(hours, few, columns)
        return carry

    lax.fori_loop(0, parts, part_of_first, 0, unroll=4)
    lat = lat_ref[...]

    def hour(t, carry):
        f = first_ref[:, t].reshape(rows, columns).astype(jnp.bfloat16)
        s = jnp.dot(lat, f, preferred_element_type=jnp.float32)
        at = pl.ds(pl.multiple_of(t * STRIDE, 8), rows)
        for k in range(3):
            width = min(LANES, columns - LANES * k)
            second_ref[k, at, :width] = s[:, LANES * k : LANES * k + width]
        return carry

    lax.fori_loop(0, hours, hour, 0, unroll=10)
    row = lax.broadcasted_iota(jnp.int32, (8, LANES), 0)
    lane8 = lax.broadcasted_iota(jnp.int32, (8, LANES), 1)
    lane = lax.broadcasted_iota(jnp.int32, (24, LANES), 1)

    def triple(p, carry):
        a, b, c = (
            jnp.concatenate(
                [second_ref[jnp.int32(k), pl.ds(jnp.int32(r * third) + p, 24, STRIDE), :] for k in range(3)], axis=1
            )
            for r in range(3)
        )
        b_up = pltpu.roll(b, 104, 1)
        out_ref[2 * p] = pack(
            [tile(a, 0), tile(a, 1), jnp.where(lane < 104, tile(a, 2), tile(b_up, 0)), tile(b_up, 1), tile(b_up, 2)],
            row,
            lane8,
        )
        b_down = pltpu.roll(b, 204, 1)
        c_up = pltpu.roll(c, 180, 1)
        out_ref[2 * p + 1] = pack(
            [
                tile(b_down, 0),
                jnp.where(lane < 52, tile(b_down, 1), tile(c_up, 1)),
                tile(c_up, 2),
                tile(c_up, 0),
                tile(c_up, 1),
            ],
            row,
            lane8,
        )
        return carry

    each = out_ref.shape[0] // COPIES

    def leave(n):
        at = pl.ds(n * each, each)
        return pltpu.make_async_copy(out_ref.at[at], to_ref.at[at], sem.at[n])

    def some(n, carry):
        lax.fori_loop(0, each // 8, lambda q, c: [triple(n * (each // 2) + 4 * q + i, c) for i in range(4)][-1], 0)
        leave(n).start()
        return carry

    lax.fori_loop(0, COPIES, some, 0)
    for n in range(COPIES):
        leave(n).wait()


def mix(x, lon, lat):
    parts, hours, few, columns = x.shape
    rows = lat.shape[0]
    return pl.pallas_call(
        mix_kernel,
        in_specs=[WHOLE] * 3,
        out_specs=OUTSIDE,
        out_shape=jax.ShapeDtypeStruct((2 * rows // 3, BLOCK, LANES), jnp.bfloat16),
        scratch_shapes=[
            pltpu.VMEM((parts, hours, few, columns), jnp.float32),
            pltpu.VMEM((3, 24 * STRIDE, LANES), jnp.float32),
            pltpu.VMEM((2 * rows // 3, BLOCK, LANES), jnp.bfloat16),
            pltpu.SemaphoreType.DMA((COPIES,)),
        ],
        compiler_params=params(24),
    )(x, lon, lat)


def order_kernel(t_ref, move_ref, out_ref):
    move = move_ref[...]
    total = t_ref.shape[1]
    main = 32 * MAIN
    tail = GROUP - main
    for u in range(total // GROUP):
        w = jnp.dot(t_ref[:, GROUP * u : GROUP * (u + 1)], move, preferred_element_type=jnp.float32).astype(jnp.bfloat16)
        out_ref[:, main * u : main * (u + 1)] = w[:, :main]
        start = total // GROUP * main + tail * u
        out_ref[:, start : start + tail] = w[:, main:]


def order_columns(time_factor):
    rows, total = time_factor.shape
    col = jnp.arange(GROUP)
    main = 32 * MAIN
    hour = jnp.where(col < main, col // MAIN * HOURS + col % MAIN, (col - main) % 32 * HOURS + MAIN + (col - main) // 32)
    move = (jnp.arange(GROUP)[:, None] == hour[None, :]).astype(jnp.bfloat16)
    few = 256
    return pl.pallas_call(
        order_kernel,
        grid=(rows // few,),
        in_specs=[pl.BlockSpec((few, total), lambda i: (i, 0)), pl.BlockSpec((GROUP, GROUP), lambda i: (0, 0))],
        out_specs=pl.BlockSpec((few, total), lambda i: (i, 0)),
        out_shape=jax.ShapeDtypeStruct((rows, total), jnp.bfloat16),
        compiler_params=params(16),
    )(time_factor, move)


def unpack(r_ref, gt_ref, tail_ref):
    sources = r_ref.shape[0]
    main = sources * MAIN
    few = BLOCK - 64
    tail_ref[...] = r_ref[:, 64:].astype(jnp.float32).reshape(sources * few, LANES)

    def tails(first):
        parts = []
        for u in range(sources // 32):
            for i in range(HOURS - MAIN):
                parts.append(tail_ref[pl.ds(u * 32 * few + first + i, 32, few), :])
        return jnp.concatenate(parts, axis=0)

    for k in range(4):
        at = slice(LANES * k, LANES * (k + 1))
        gt_ref[at, :main] = r_ref[:, 16 * k : 16 * k + 16].reshape(main, LANES).T
        gt_ref[at, main:] = tails(4 * k).T.astype(jnp.bfloat16)
    at = slice(4 * LANES, TALL)
    last = r_ref[:, 80:88].astype(jnp.float32).reshape(sources * 8, LANES)
    both = jnp.concatenate(
        [last.reshape(sources, 1, 8, LANES), pltpu.roll(last, 96, 1).reshape(sources, 1, 8, LANES)], axis=1
    )
    gt_ref[at, :main] = both.reshape(main, LANES).T[: TALL - 4 * LANES].astype(jnp.bfloat16)
    gt_ref[at, main:] = pltpu.roll(tails(16), 64, 1).T[: TALL - 4 * LANES].astype(jnp.bfloat16)


def time_kernel(r_ref, t_ref, out_ref, gt_ref, tail_ref, held_ref, sem):
    few = out_ref.shape[1]
    step = pl.program_id(0)

    def arrival(n):
        at = pl.ds(pl.multiple_of(n * few, few), few)
        return pltpu.make_async_copy(t_ref.at[at], held_ref.at[at], sem.at[n])

    @pl.when(step == 0)
    def _():
        arrival(0).start()
        arrival(1).start()
        unpack(r_ref, gt_ref, tail_ref)

    @pl.when(step + 2 < pl.num_programs(0))
    def _():
        arrival(step + 2).start()

    arrival(step).wait()
    t = held_ref[pl.ds(pl.multiple_of(step * few, few), few), :]
    w = lax.dot_general(gt_ref[...], t, (((1,), (1,)), ((), ())), preferred_element_type=jnp.float32)
    out_ref[...] = w[:CELLS].astype(jnp.bfloat16)


def time_product(r, t):
    few = 512
    out_rows, total = t.shape
    return pl.pallas_call(
        time_kernel,
        grid=(out_rows // few,),
        in_specs=[WHOLE, OUTSIDE],
        out_specs=pl.BlockSpec((CELLS, few), lambda i: (0, i)),
        out_shape=jax.ShapeDtypeStruct((CELLS, out_rows), jnp.bfloat16),
        scratch_shapes=[
            pltpu.VMEM((TALL, total), jnp.bfloat16),
            pltpu.VMEM((r.shape[0] * (BLOCK - 64), LANES), jnp.float32),
            pltpu.VMEM((out_rows, total), jnp.bfloat16),
            pltpu.SemaphoreType.DMA((out_rows // few,)),
        ],
        compiler_params=params(40),
    )(r, t)


def by_thirds(lat_factor):
    rows = lat_factor.shape[0]
    return lat_factor.reshape(rows // 3, 3, rows).transpose(1, 0, 2).reshape(rows, rows)


def on_device(field, time_factor, lat_factor, lon_factor):
    hours, few, columns = field.shape
    parts = lax.axis_size("lat")
    moved = lax.all_to_all(field, "lat", split_axis=0, concat_axis=0, tiled=True)
    ordered = order_columns(time_factor)
    lat = by_thirds(lat_factor)
    blocks = mix(moved.reshape(parts, hours // parts, few, columns), lon_factor, lat)
    got = lax.all_to_all(blocks, ("tm", "lat"), split_axis=0, concat_axis=0, tiled=True)
    return time_product(got, ordered).T


def solution(mesh):
    return jax.shard_map(
        on_device,
        mesh=mesh,
        in_specs=(P("tm", "lat", None), P(), P(), P()),
        out_specs=P(None, ("tm", "lat")),
        check_vma=False,
    )
```

```python
import jax
import jax.numpy as jnp
from jax import lax
from jax.experimental import pallas as pl
from jax.experimental.pallas import tpu as pltpu
from jax.sharding import PartitionSpec as P

LANES = 128
CELLS = 540
TALL = 544
HOURS = 20
MAIN = 16
BLOCK = 88
GROUP = 32 * HOURS
STRIDE = 200
COPIES = 8
WHOLE = pl.BlockSpec(memory_space=pltpu.VMEM)
OUTSIDE = pl.BlockSpec(memory_space=pltpu.HBM)


def params(mib):
    return pltpu.CompilerParams(vmem_limit_bytes=mib * 1024 * 1024)


def tile(v, k):
    return v[:, LANES * k : LANES * (k + 1)]


def pack(tiles, row, lane):
    tails = [jnp.where(row < 4, tiles[k][16:], pltpu.roll(tiles[k + 1][16:], 4, 0)) for k in (0, 2)]
    rest = tiles[4]
    last = jnp.where(
        lane < 32,
        rest[:8],
        jnp.where(lane < 64, pltpu.roll(rest[8:16], 32, 1), pltpu.roll(rest[16:], 64, 1)),
    )
    return jnp.concatenate([t[:16] for t in tiles[:4]] + tails + [last], axis=0).astype(jnp.bfloat16)


def mix_kernel(x_ref, lon_ref, lat_ref, to_ref, first_ref, second_ref, out_ref, sem):
    parts, hours, few, columns = x_ref.shape
    rows = parts * few
    third = rows // 3
    lon = lon_ref[...]

    def part_of_first(part, carry):
        x = x_ref[part].astype(jnp.float32).reshape(hours * few, columns).astype(jnp.bfloat16)
        first = jnp.dot(x, lon, preferred_element_type=jnp.float32)
        first_ref[part] = first.reshape(hours, few, columns)
        return carry

    lax.fori_loop(0, parts, part_of_first, 0, unroll=4)
    lat = lat_ref[...]

    def hour(t, carry):
        f = first_ref[:, t].reshape(rows, columns).astype(jnp.bfloat16)
        s = jnp.dot(lat, f, preferred_element_type=jnp.float32)
        at = pl.ds(pl.multiple_of(t * STRIDE, 8), rows)
        for k in range(3):
            width = min(LANES, columns - LANES * k)
            second_ref[k, at, :width] = s[:, LANES * k : LANES * k + width]
        return carry

    lax.fori_loop(0, hours, hour, 0, unroll=10)
    row = lax.broadcasted_iota(jnp.int32, (8, LANES), 0)
    lane8 = lax.broadcasted_iota(jnp.int32, (8, LANES), 1)
    lane = lax.broadcasted_iota(jnp.int32, (24, LANES), 1)

    def triple(p, carry):
        a, b, c = (
            jnp.concatenate(
                [second_ref[jnp.int32(k), pl.ds(jnp.int32(r * third) + p, 24, STRIDE), :] for k in range(3)], axis=1
            )
            for r in range(3)
        )
        b_up = pltpu.roll(b, 104, 1)
        out_ref[2 * p] = pack(
            [tile(a, 0), tile(a, 1), jnp.where(lane < 104, tile(a, 2), tile(b_up, 0)), tile(b_up, 1), tile(b_up, 2)],
            row,
            lane8,
        )
        b_down = pltpu.roll(b, 204, 1)
        c_up = pltpu.roll(c, 180, 1)
        out_ref[2 * p + 1] = pack(
            [
                tile(b_down, 0),
                jnp.where(lane < 52, tile(b_down, 1), tile(c_up, 1)),
                tile(c_up, 2),
                tile(c_up, 0),
                tile(c_up, 1),
            ],
            row,
            lane8,
        )
        return carry

    each = out_ref.shape[0] // COPIES

    def leave(n):
        at = pl.ds(n * each, each)
        return pltpu.make_async_copy(out_ref.at[at], to_ref.at[at], sem.at[n])

    def some(n, carry):
        lax.fori_loop(0, each // 8, lambda q, c: [triple(n * (each // 2) + 4 * q + i, c) for i in range(4)][-1], 0)
        leave(n).start()
        return carry

    lax.fori_loop(0, COPIES, some, 0)
    for n in range(COPIES):
        leave(n).wait()


def mix(x, lon, lat):
    parts, hours, few, columns = x.shape
    rows = lat.shape[0]
    return pl.pallas_call(
        mix_kernel,
        in_specs=[WHOLE] * 3,
        out_specs=OUTSIDE,
        out_shape=pltpu.HBM((2 * rows // 3, BLOCK, LANES), jnp.bfloat16),
        scratch_shapes=[
            pltpu.VMEM((parts, hours, few, columns), jnp.float32),
            pltpu.VMEM((3, 24 * STRIDE, LANES), jnp.float32),
            pltpu.VMEM((2 * rows // 3, BLOCK, LANES), jnp.bfloat16),
            pltpu.SemaphoreType.DMA((COPIES,)),
        ],
        compiler_params=params(24),
    )(x, lon, lat)


def order_kernel(t_ref, move_ref, out_ref):
    move = move_ref[...]
    total = t_ref.shape[1]
    main = 32 * MAIN
    tail = GROUP - main
    for u in range(total // GROUP):
        w = jnp.dot(t_ref[:, GROUP * u : GROUP * (u + 1)], move, preferred_element_type=jnp.float32).astype(jnp.bfloat16)
        out_ref[:, main * u : main * (u + 1)] = w[:, :main]
        start = total // GROUP * main + tail * u
        out_ref[:, start : start + tail] = w[:, main:]


def order_columns(time_factor):
    rows, total = time_factor.shape
    col = jnp.arange(GROUP)
    main = 32 * MAIN
    hour = jnp.where(col < main, col // MAIN * HOURS + col % MAIN, (col - main) % 32 * HOURS + MAIN + (col - main) // 32)
    move = (jnp.arange(GROUP)[:, None] == hour[None, :]).astype(jnp.bfloat16)
    few = 256
    return pl.pallas_call(
        order_kernel,
        grid=(rows // few,),
        in_specs=[pl.BlockSpec((few, total), lambda i: (i, 0)), pl.BlockSpec((GROUP, GROUP), lambda i: (0, 0))],
        out_specs=pl.BlockSpec((few, total), lambda i: (i, 0)),
        out_shape=jax.ShapeDtypeStruct((rows, total), jnp.bfloat16),
        compiler_params=params(16),
    )(time_factor, move)


def unpack(r_ref, gt_ref, tail_ref):
    sources = r_ref.shape[0]
    main = sources * MAIN
    few = BLOCK - 64
    tail_ref[...] = r_ref[:, 64:].astype(jnp.float32).reshape(sources * few, LANES)

    def tails(first):
        parts = []
        for u in range(sources // 32):
            for i in range(HOURS - MAIN):
                parts.append(tail_ref[pl.ds(u * 32 * few + first + i, 32, few), :])
        return jnp.concatenate(parts, axis=0)

    for k in range(4):
        at = slice(LANES * k, LANES * (k + 1))
        gt_ref[at, :main] = r_ref[:, 16 * k : 16 * k + 16].reshape(main, LANES).T
        gt_ref[at, main:] = tails(4 * k).T.astype(jnp.bfloat16)
    at = slice(4 * LANES, TALL)
    last = r_ref[:, 80:88].astype(jnp.float32).reshape(sources * 8, LANES)
    both = jnp.concatenate(
        [last.reshape(sources, 1, 8, LANES), pltpu.roll(last, 96, 1).reshape(sources, 1, 8, LANES)], axis=1
    )
    gt_ref[at, :main] = both.reshape(main, LANES).T[: TALL - 4 * LANES].astype(jnp.bfloat16)
    gt_ref[at, main:] = pltpu.roll(tails(16), 64, 1).T[: TALL - 4 * LANES].astype(jnp.bfloat16)


def time_kernel(r_ref, t_ref, out_ref, gt_ref, tail_ref, held_ref, sem):
    few = out_ref.shape[1]
    step = pl.program_id(0)

    def arrival(n):
        at = pl.ds(pl.multiple_of(n * few, few), few)
        return pltpu.make_async_copy(t_ref.at[at], held_ref.at[at], sem.at[n])

    @pl.when(step == 0)
    def _():
        arrival(0).start()
        arrival(1).start()
        unpack(r_ref, gt_ref, tail_ref)

    @pl.when(step + 2 < pl.num_programs(0))
    def _():
        arrival(step + 2).start()

    arrival(step).wait()
    t = held_ref[pl.ds(pl.multiple_of(step * few, few), few), :]
    w = lax.dot_general(gt_ref[...], t, (((1,), (1,)), ((), ())), preferred_element_type=jnp.float32)
    out_ref[...] = w[:CELLS].astype(jnp.bfloat16)


def time_product(r, t):
    few = 512
    out_rows, total = t.shape
    return pl.pallas_call(
        time_kernel,
        grid=(out_rows // few,),
        in_specs=[WHOLE, OUTSIDE],
        out_specs=pl.BlockSpec((CELLS, few), lambda i: (0, i)),
        out_shape=jax.ShapeDtypeStruct((CELLS, out_rows), jnp.bfloat16),
        scratch_shapes=[
            pltpu.VMEM((TALL, total), jnp.bfloat16),
            pltpu.VMEM((r.shape[0] * (BLOCK - 64), LANES), jnp.float32),
            pltpu.VMEM((out_rows, total), jnp.bfloat16),
            pltpu.SemaphoreType.DMA((out_rows // few,)),
        ],
        compiler_params=params(40),
    )(r, t)


def by_thirds(lat_factor):
    rows = lat_factor.shape[0]
    return lat_factor.reshape(rows // 3, 3, rows).transpose(1, 0, 2).reshape(rows, rows)


def on_device(field, time_factor, lat_factor, lon_factor):
    hours, few, columns = field.shape
    parts = lax.axis_size("lat")
    moved = lax.all_to_all(field, "lat", split_axis=0, concat_axis=0, tiled=True)
    ordered = order_columns(time_factor)
    lat = by_thirds(lat_factor)
    blocks = mix(moved.reshape(parts, hours // parts, few, columns), lon_factor, lat)
    got = lax.all_to_all(blocks, ("tm", "lat"), split_axis=0, concat_axis=0, tiled=True)
    return time_product(got, ordered).T


def solution(mesh):
    return jax.shard_map(
        on_device,
        mesh=mesh,
        in_specs=(P("tm", "lat", None), P(), P(), P()),
        out_specs=P(None, ("tm", "lat")),
        check_vma=False,
    )
```

```python
import jax
import jax.numpy as jnp
from jax import lax
from jax.experimental import pallas as pl
from jax.experimental.pallas import tpu as pltpu
from jax.sharding import PartitionSpec as P

LANES = 128
CELLS = 540
TALL = 544
HOURS = 20
MAIN = 16
BLOCK = 88
GROUP = 32 * HOURS
STRIDE = 200
COPIES = 8
WHOLE = pl.BlockSpec(memory_space=pltpu.VMEM)
OUTSIDE = pl.BlockSpec(memory_space=pltpu.HBM)


def params(mib):
    return pltpu.CompilerParams(vmem_limit_bytes=mib * 1024 * 1024)


def tile(v, k):
    return v[:, LANES * k : LANES * (k + 1)]


def pack(tiles, row, lane):
    tails = [jnp.where(row < 4, tiles[k][16:], pltpu.roll(tiles[k + 1][16:], 4, 0)) for k in (0, 2)]
    rest = tiles[4]
    last = jnp.where(
        lane < 32,
        rest[:8],
        jnp.where(lane < 64, pltpu.roll(rest[8:16], 32, 1), pltpu.roll(rest[16:], 64, 1)),
    )
    return jnp.concatenate([t[:16] for t in tiles[:4]] + tails + [last], axis=0).astype(jnp.bfloat16)


def mix_kernel(x_ref, lon_ref, lat_ref, to_ref, first_ref, second_ref, out_ref, sem):
    parts, hours, few, columns = x_ref.shape
    rows = parts * few
    third = rows // 3
    lon = lon_ref[...]

    def part_of_first(part, carry):
        x = x_ref[part].astype(jnp.float32).reshape(hours * few, columns).astype(jnp.bfloat16)
        first = jnp.dot(x, lon, preferred_element_type=jnp.float32)
        first_ref[part] = first.reshape(hours, few, columns)
        return carry

    lax.fori_loop(0, parts, part_of_first, 0, unroll=4)
    lat = lat_ref[...]

    def hour(t, carry):
        f = first_ref[:, t].reshape(rows, columns).astype(jnp.bfloat16)
        s = jnp.dot(lat, f, preferred_element_type=jnp.float32)
        at = pl.ds(pl.multiple_of(t * STRIDE, 8), rows)
        for k in range(3):
            width = min(LANES, columns - LANES * k)
            second_ref[k, at, :width] = s[:, LANES * k : LANES * k + width]
        return carry

    lax.fori_loop(0, hours, hour, 0, unroll=10)
    row = lax.broadcasted_iota(jnp.int32, (8, LANES), 0)
    lane8 = lax.broadcasted_iota(jnp.int32, (8, LANES), 1)
    lane = lax.broadcasted_iota(jnp.int32, (24, LANES), 1)

    def triple(p, even, odd):
        a, b, c = (
            jnp.concatenate(
                [second_ref[jnp.int32(k), pl.ds(jnp.int32(r * third) + p, 24, STRIDE), :] for k in range(3)], axis=1
            )
            for r in range(3)
        )
        b_up = pltpu.roll(b, 104, 1)
        out_ref[even] = pack(
            [tile(a, 0), tile(a, 1), jnp.where(lane < 104, tile(a, 2), tile(b_up, 0)), tile(b_up, 1), tile(b_up, 2)],
            row,
            lane8,
        )
        b_down = pltpu.roll(b, 204, 1)
        c_up = pltpu.roll(c, 180, 1)
        out_ref[odd] = pack(
            [
                tile(b_down, 0),
                jnp.where(lane < 52, tile(b_down, 1), tile(c_up, 1)),
                tile(c_up, 2),
                tile(c_up, 0),
                tile(c_up, 1),
            ],
            row,
            lane8,
        )

    each = out_ref.shape[0] // COPIES

    def leave(n):
        at = pl.ds(n * each, each)
        return pltpu.make_async_copy(out_ref.at[at], to_ref.at[at], sem.at[n])

    def some(n, carry):
        core, z = n // 4, n % 4

        def four(x_lo, inner):
            for i in range(4):
                x_hi, y = i // 2, i % 2 * 2
                at = n * each + y * 4 + x_hi * 2 + x_lo
                triple(z * 16 + x_lo * 8 + core * 4 + i, at, at + 4)
            return inner

        lax.fori_loop(0, 2, four, 0)
        leave(n).start()
        return carry

    lax.fori_loop(0, COPIES, some, 0)
    for n in range(COPIES):
        leave(n).wait()


def mix(x, lon, lat):
    parts, hours, few, columns = x.shape
    rows = lat.shape[0]
    return pl.pallas_call(
        mix_kernel,
        in_specs=[WHOLE] * 3,
        out_specs=OUTSIDE,
        out_shape=pltpu.HBM((2 * rows // 3, BLOCK, LANES), jnp.bfloat16),
        scratch_shapes=[
            pltpu.VMEM((parts, hours, few, columns), jnp.float32),
            pltpu.VMEM((3, 24 * STRIDE, LANES), jnp.float32),
            pltpu.VMEM((2 * rows // 3, BLOCK, LANES), jnp.bfloat16),
            pltpu.SemaphoreType.DMA((COPIES,)),
        ],
        compiler_params=params(24),
    )(x, lon, lat)


def order_kernel(t_ref, move_ref, out_ref):
    move = move_ref[...]
    total = t_ref.shape[1]
    groups = total // GROUP
    main, tail = 16 * MAIN, 16 * (HOURS - MAIN)
    tails = []
    for z in range(groups):
        w = jnp.dot(t_ref[:, GROUP * z : GROUP * (z + 1)], move, preferred_element_type=jnp.float32)
        for core in range(2):
            at = (core * groups + z) * main
            out_ref[:, at : at + main] = w[:, main * core : main * (core + 1)].astype(jnp.bfloat16)
        tails.append(w[:, 2 * main :])
    low = lax.broadcasted_iota(jnp.int32, tails[0].shape, 1) < tail
    start = 2 * groups * main
    for z in range(0, groups, 2):
        x, y = tails[z], tails[z + 1]
        for core, both in enumerate((jnp.where(low, x, pltpu.roll(y, tail, 1)), jnp.where(low, pltpu.roll(x, tail, 1), y))):
            at = start + (core * groups + z) * tail
            out_ref[:, at : at + 2 * tail] = both.astype(jnp.bfloat16)


def order_columns(time_factor):
    rows, total = time_factor.shape
    col = jnp.arange(GROUP)
    main, tail = 16 * MAIN, 16 * (HOURS - MAIN)
    late = col >= 2 * main
    core = jnp.where(late, (col - 2 * main) // tail, col // main)
    within = jnp.where(late, (col - 2 * main) % tail, col % main)
    device = jnp.where(late, within % 16, within // MAIN)
    which = jnp.where(late, MAIN + within // 16, within % MAIN)
    y, x_hi, x_lo = device // 4, device // 2 % 2, device % 2
    hour = (x_lo * 2 + core) * 8 * HOURS + (x_hi * 4 + y) * HOURS + which
    move = (jnp.arange(GROUP)[:, None] == hour[None, :]).astype(jnp.bfloat16)
    few = 256
    return pl.pallas_call(
        order_kernel,
        grid=(rows // few,),
        in_specs=[pl.BlockSpec((few, total), lambda i: (i, 0)), pl.BlockSpec((GROUP, GROUP), lambda i: (0, 0))],
        out_specs=pl.BlockSpec((few, total), lambda i: (i, 0)),
        out_shape=jax.ShapeDtypeStruct((rows, total), jnp.bfloat16),
        compiler_params=params(16),
    )(time_factor, move)


def unpack(r_ref, gt_ref, tail_ref):
    sources = r_ref.shape[0]
    main = sources * MAIN
    few = BLOCK - 64
    tail_ref[...] = r_ref[:, 64:].astype(jnp.float32).reshape(sources * few, LANES)

    def tails(first):
        parts = []
        for u in range(sources // 16):
            for i in range(HOURS - MAIN):
                parts.append(tail_ref[pl.ds(u * 16 * few + first + i, 16, few), :])
        return jnp.concatenate(parts, axis=0)

    for k in range(4):
        at = slice(LANES * k, LANES * (k + 1))
        gt_ref[at, :main] = r_ref[:, 16 * k : 16 * k + 16].reshape(main, LANES).T
        gt_ref[at, main:] = tails(4 * k).T.astype(jnp.bfloat16)
    at = slice(4 * LANES, TALL)
    last = r_ref[:, 80:88].astype(jnp.float32).reshape(sources * 8, LANES)
    both = jnp.concatenate(
        [last.reshape(sources, 1, 8, LANES), pltpu.roll(last, 96, 1).reshape(sources, 1, 8, LANES)], axis=1
    )
    gt_ref[at, :main] = both.reshape(main, LANES).T[: TALL - 4 * LANES].astype(jnp.bfloat16)
    gt_ref[at, main:] = pltpu.roll(tails(16), 64, 1).T[: TALL - 4 * LANES].astype(jnp.bfloat16)


def time_kernel(r_ref, t_ref, out_ref, gt_ref, tail_ref, held_ref, sem):
    few = out_ref.shape[1]
    step = pl.program_id(0)

    def arrival(n):
        at = pl.ds(pl.multiple_of(n * few, few), few)
        return pltpu.make_async_copy(t_ref.at[at], held_ref.at[at], sem.at[n])

    @pl.when(step == 0)
    def _():
        arrival(0).start()
        arrival(1).start()
        unpack(r_ref, gt_ref, tail_ref)

    @pl.when(step + 2 < pl.num_programs(0))
    def _():
        arrival(step + 2).start()

    arrival(step).wait()
    t = held_ref[pl.ds(pl.multiple_of(step * few, few), few), :]
    w = lax.dot_general(gt_ref[...], t, (((1,), (1,)), ((), ())), preferred_element_type=jnp.float32)
    out_ref[...] = w[:CELLS].astype(jnp.bfloat16)


def time_product(r, t):
    few = 512
    out_rows, total = t.shape
    return pl.pallas_call(
        time_kernel,
        grid=(out_rows // few,),
        in_specs=[WHOLE, OUTSIDE],
        out_specs=pl.BlockSpec((CELLS, few), lambda i: (0, i)),
        out_shape=jax.ShapeDtypeStruct((CELLS, out_rows), jnp.bfloat16),
        scratch_shapes=[
            pltpu.VMEM((TALL, total), jnp.bfloat16),
            pltpu.VMEM((r.shape[0] * (BLOCK - 64), LANES), jnp.float32),
            pltpu.VMEM((out_rows, total), jnp.bfloat16),
            pltpu.SemaphoreType.DMA((out_rows // few,)),
        ],
        compiler_params=params(40),
    )(r, t)


def by_thirds(lat_factor):
    rows = lat_factor.shape[0]
    return lat_factor.reshape(rows // 3, 3, rows).transpose(1, 0, 2).reshape(rows, rows)


def on_device(field, time_factor, lat_factor, lon_factor):
    hours, few, columns = field.shape
    parts = lax.axis_size(("x_hi", "y"))
    moved = lax.all_to_all(field, ("x_hi", "y"), split_axis=0, concat_axis=0, tiled=True)
    ordered = order_columns(time_factor)
    lat = by_thirds(lat_factor)
    blocks = mix(moved.reshape(parts, hours // parts, few, columns), lon_factor, lat)
    got = lax.all_to_all(blocks, ("core", "z", "y", "x_hi", "x_lo"), split_axis=0, concat_axis=0, tiled=True)
    return time_product(got, ordered).T


def solution(mesh):
    tm, lat = ("z", "x_lo", "core"), ("x_hi", "y")
    parts = jax.sharding.Mesh(mesh.devices.reshape(4, 2, 2, 2, 4), tm + lat)
    return jax.shard_map(
        on_device,
        mesh=parts,
        in_specs=(P(tm, lat, None), P(), P(), P()),
        out_specs=P(None, tm + lat),
        check_vma=False,
    )
```

```python
import jax
import jax.numpy as jnp
from jax import lax
from jax.experimental import pallas as pl
from jax.experimental.pallas import tpu as pltpu
from jax.sharding import PartitionSpec as P

LANES = 128
CELLS = 540
TALL = 544
HOURS = 20
MAIN = 16
BLOCK = 88
GROUP = 32 * HOURS
STRIDE = 200
COPIES = 8
WHOLE = pl.BlockSpec(memory_space=pltpu.VMEM)
OUTSIDE = pl.BlockSpec(memory_space=pltpu.HBM)


def params(mib):
    return pltpu.CompilerParams(vmem_limit_bytes=mib * 1024 * 1024)


def tile(v, k):
    return v[:, LANES * k : LANES * (k + 1)]


def pack(tiles, row, lane):
    tails = [jnp.where(row < 4, tiles[k][16:], pltpu.roll(tiles[k + 1][16:], 4, 0)) for k in (0, 2)]
    rest = tiles[4]
    last = jnp.where(
        lane < 32,
        rest[:8],
        jnp.where(lane < 64, pltpu.roll(rest[8:16], 32, 1), pltpu.roll(rest[16:], 64, 1)),
    )
    return jnp.concatenate([t[:16] for t in tiles[:4]] + tails + [last], axis=0).astype(jnp.bfloat16)


def mix_kernel(x_ref, lon_ref, lat_ref, to_ref, first_ref, second_ref, out_ref, sem):
    parts, hours, few, columns = x_ref.shape
    rows = parts * few
    third = rows // 3
    lon = lon_ref[...]

    def part_of_first(part, carry):
        x = x_ref[part].astype(jnp.float32).reshape(hours * few, columns).astype(jnp.bfloat16)
        first = jnp.dot(x, lon, preferred_element_type=jnp.float32)
        first_ref[part] = first.reshape(hours, few, columns)
        return carry

    lax.fori_loop(0, parts, part_of_first, 0, unroll=8)
    lat = lat_ref[...]

    def hour(t, carry):
        f = first_ref[:, t].reshape(rows, columns).astype(jnp.bfloat16)
        s = jnp.dot(lat, f, preferred_element_type=jnp.float32)
        at = pl.ds(pl.multiple_of(t * STRIDE, 8), rows)
        for k in range(3):
            width = min(LANES, columns - LANES * k)
            second_ref[k, at, :width] = s[:, LANES * k : LANES * k + width]
        return carry

    lax.fori_loop(0, hours, hour, 0, unroll=20)
    row = lax.broadcasted_iota(jnp.int32, (8, LANES), 0)
    lane8 = lax.broadcasted_iota(jnp.int32, (8, LANES), 1)
    lane = lax.broadcasted_iota(jnp.int32, (24, LANES), 1)

    def triple(p, even, odd):
        a, b, c = (
            jnp.concatenate(
                [second_ref[jnp.int32(k), pl.ds(jnp.int32(r * third) + p, 24, STRIDE), :] for k in range(3)], axis=1
            )
            for r in range(3)
        )
        b_up = pltpu.roll(b, 104, 1)
        out_ref[even] = pack(
            [tile(a, 0), tile(a, 1), jnp.where(lane < 104, tile(a, 2), tile(b_up, 0)), tile(b_up, 1), tile(b_up, 2)],
            row,
            lane8,
        )
        b_down = pltpu.roll(b, 204, 1)
        c_up = pltpu.roll(c, 180, 1)
        out_ref[odd] = pack(
            [
                tile(b_down, 0),
                jnp.where(lane < 52, tile(b_down, 1), tile(c_up, 1)),
                tile(c_up, 2),
                tile(c_up, 0),
                tile(c_up, 1),
            ],
            row,
            lane8,
        )

    each = out_ref.shape[0] // COPIES

    def leave(n):
        at = pl.ds(n * each, each)
        return pltpu.make_async_copy(out_ref.at[at], to_ref.at[at], sem.at[n])

    def some(n, carry):
        core, z = n // 4, n % 4

        def four(x_lo, inner):
            for i in range(4):
                x_hi, y = i // 2, i % 2 * 2
                at = n * each + y * 4 + x_hi * 2 + x_lo
                triple(z * 16 + x_lo * 8 + core * 4 + i, at, at + 4)
            return inner

        lax.fori_loop(0, 2, four, 0)
        leave(n).start()
        return carry

    lax.fori_loop(0, COPIES, some, 0)
    for n in range(COPIES):
        leave(n).wait()


def mix(x, lon, lat):
    parts, hours, few, columns = x.shape
    rows = lat.shape[0]
    return pl.pallas_call(
        mix_kernel,
        in_specs=[WHOLE] * 3,
        out_specs=OUTSIDE,
        out_shape=pltpu.HBM((2 * rows // 3, BLOCK, LANES), jnp.bfloat16),
        scratch_shapes=[
            pltpu.VMEM((parts, hours, few, columns), jnp.float32),
            pltpu.VMEM((3, 24 * STRIDE, LANES), jnp.float32),
            pltpu.VMEM((2 * rows // 3, BLOCK, LANES), jnp.bfloat16),
            pltpu.SemaphoreType.DMA((COPIES,)),
        ],
        compiler_params=params(24),
    )(x, lon, lat)


def order_kernel(t_ref, move_ref, out_ref):
    move = move_ref[...]
    total = t_ref.shape[1]
    groups = total // GROUP
    main, tail = 16 * MAIN, 16 * (HOURS - MAIN)
    tails = []
    for z in range(groups):
        w = jnp.dot(t_ref[:, GROUP * z : GROUP * (z + 1)], move, preferred_element_type=jnp.float32)
        for core in range(2):
            at = (core * groups + z) * main
            out_ref[:, at : at + main] = w[:, main * core : main * (core + 1)].astype(jnp.bfloat16)
        tails.append(w[:, 2 * main :])
    low = lax.broadcasted_iota(jnp.int32, tails[0].shape, 1) < tail
    start = 2 * groups * main
    for z in range(0, groups, 2):
        x, y = tails[z], tails[z + 1]
        for core, both in enumerate((jnp.where(low, x, pltpu.roll(y, tail, 1)), jnp.where(low, pltpu.roll(x, tail, 1), y))):
            at = start + (core * groups + z) * tail
            out_ref[:, at : at + 2 * tail] = both.astype(jnp.bfloat16)


def order_columns(time_factor):
    rows, total = time_factor.shape
    col = jnp.arange(GROUP)
    main, tail = 16 * MAIN, 16 * (HOURS - MAIN)
    late = col >= 2 * main
    core = jnp.where(late, (col - 2 * main) // tail, col // main)
    within = jnp.where(late, (col - 2 * main) % tail, col % main)
    device = jnp.where(late, within % 16, within // MAIN)
    which = jnp.where(late, MAIN + within // 16, within % MAIN)
    y, x_hi, x_lo = device // 4, device // 2 % 2, device % 2
    hour = (x_lo * 2 + core) * 8 * HOURS + (x_hi * 4 + y) * HOURS + which
    move = (jnp.arange(GROUP)[:, None] == hour[None, :]).astype(jnp.bfloat16)
    few = 256
    return pl.pallas_call(
        order_kernel,
        grid=(rows // few,),
        in_specs=[pl.BlockSpec((few, total), lambda i: (i, 0)), pl.BlockSpec((GROUP, GROUP), lambda i: (0, 0))],
        out_specs=pl.BlockSpec((few, total), lambda i: (i, 0)),
        out_shape=jax.ShapeDtypeStruct((rows, total), jnp.bfloat16),
        compiler_params=params(16),
    )(time_factor, move)


def unpack(r_ref, gt_ref, tail_ref):
    sources = r_ref.shape[0]
    main = sources * MAIN
    few = BLOCK - 64
    tail_ref[...] = r_ref[:, 64:].astype(jnp.float32).reshape(sources * few, LANES)

    def tails(first):
        parts = []
        for u in range(sources // 16):
            for i in range(HOURS - MAIN):
                parts.append(tail_ref[pl.ds(u * 16 * few + first + i, 16, few), :])
        return jnp.concatenate(parts, axis=0)

    for k in range(4):
        at = slice(LANES * k, LANES * (k + 1))
        gt_ref[at, :main] = r_ref[:, 16 * k : 16 * k + 16].reshape(main, LANES).T
        gt_ref[at, main:] = tails(4 * k).T.astype(jnp.bfloat16)
    at = slice(4 * LANES, TALL)
    last = r_ref[:, 80:88].astype(jnp.float32).reshape(sources * 8, LANES)
    both = jnp.concatenate(
        [last.reshape(sources, 1, 8, LANES), pltpu.roll(last, 96, 1).reshape(sources, 1, 8, LANES)], axis=1
    )
    gt_ref[at, :main] = both.reshape(main, LANES).T[: TALL - 4 * LANES].astype(jnp.bfloat16)
    gt_ref[at, main:] = pltpu.roll(tails(16), 64, 1).T[: TALL - 4 * LANES].astype(jnp.bfloat16)


def time_kernel(r_ref, t_ref, out_ref, gt_ref, tail_ref, held_ref, sem):
    few = out_ref.shape[1]
    step = pl.program_id(0)

    def arrival(n):
        at = pl.ds(pl.multiple_of(n * few, few), few)
        return pltpu.make_async_copy(t_ref.at[at], held_ref.at[at], sem.at[n])

    @pl.when(step == 0)
    def _():
        arrival(0).start()
        arrival(1).start()
        unpack(r_ref, gt_ref, tail_ref)

    @pl.when(step + 2 < pl.num_programs(0))
    def _():
        arrival(step + 2).start()

    arrival(step).wait()
    t = held_ref[pl.ds(pl.multiple_of(step * few, few), few), :]
    w = lax.dot_general(gt_ref[...], t, (((1,), (1,)), ((), ())), preferred_element_type=jnp.float32)
    out_ref[...] = w[:CELLS].astype(jnp.bfloat16)


def time_product(r, t):
    few = 512
    out_rows, total = t.shape
    return pl.pallas_call(
        time_kernel,
        grid=(out_rows // few,),
        in_specs=[WHOLE, OUTSIDE],
        out_specs=pl.BlockSpec((CELLS, few), lambda i: (0, i)),
        out_shape=jax.ShapeDtypeStruct((CELLS, out_rows), jnp.bfloat16),
        scratch_shapes=[
            pltpu.VMEM((TALL, total), jnp.bfloat16),
            pltpu.VMEM((r.shape[0] * (BLOCK - 64), LANES), jnp.float32),
            pltpu.VMEM((out_rows, total), jnp.bfloat16),
            pltpu.SemaphoreType.DMA((out_rows // few,)),
        ],
        compiler_params=params(40),
    )(r, t)


def by_thirds(lat_factor):
    rows = lat_factor.shape[0]
    return lat_factor.reshape(rows // 3, 3, rows).transpose(1, 0, 2).reshape(rows, rows)


def on_device(field, time_factor, lat_factor, lon_factor):
    hours, few, columns = field.shape
    parts = lax.axis_size(("x_hi", "y"))
    moved = lax.all_to_all(field, ("x_hi", "y"), split_axis=0, concat_axis=0, tiled=True)
    ordered = order_columns(time_factor)
    lat = by_thirds(lat_factor)
    blocks = mix(moved.reshape(parts, hours // parts, few, columns), lon_factor, lat)
    got = lax.all_to_all(blocks, ("core", "z", "y", "x_hi", "x_lo"), split_axis=0, concat_axis=0, tiled=True)
    return time_product(got, ordered).T


def solution(mesh):
    tm, lat = ("z", "x_lo", "core"), ("x_hi", "y")
    parts = jax.sharding.Mesh(mesh.devices.reshape(4, 2, 2, 2, 4), tm + lat)
    return jax.shard_map(
        on_device,
        mesh=parts,
        in_specs=(P(tm, lat, None), P(), P(), P()),
        out_specs=P(None, tm + lat),
        check_vma=False,
    )
```

```python
import jax
import jax.numpy as jnp
from jax import lax
from jax.experimental import pallas as pl
from jax.experimental.pallas import tpu as pltpu
from jax.sharding import PartitionSpec as P

LANES = 128
CELLS = 540
TALL = 544
HOURS = 20
MAIN = 16
BLOCK = 88
GROUP = 32 * HOURS
STRIDE = 200
COPIES = 8
WHOLE = pl.BlockSpec(memory_space=pltpu.VMEM)
OUTSIDE = pl.BlockSpec(memory_space=pltpu.HBM)


def params(mib):
    return pltpu.CompilerParams(vmem_limit_bytes=mib * 1024 * 1024)


def tile(v, k):
    return v[:, LANES * k : LANES * (k + 1)]


def pack(tiles, row, lane):
    tails = [jnp.where(row < 4, tiles[k][16:], pltpu.roll(tiles[k + 1][16:], 4, 0)) for k in (0, 2)]
    rest = tiles[4]
    last = jnp.where(
        lane < 32,
        rest[:8],
        jnp.where(lane < 64, pltpu.roll(rest[8:16], 32, 1), pltpu.roll(rest[16:], 64, 1)),
    )
    return jnp.concatenate([t[:16] for t in tiles[:4]] + tails + [last], axis=0).astype(jnp.bfloat16)


def mix_kernel(x_ref, lon_ref, lat_ref, to_ref, first_ref, second_ref, out_ref, sem):
    parts, hours, few, columns = x_ref.shape
    rows = parts * few
    third = rows // 3
    lon = lon_ref[...]

    def part_of_first(part, carry):
        x = x_ref[part].astype(jnp.float32).reshape(hours * few, columns).astype(jnp.bfloat16)
        first = jnp.dot(x, lon, preferred_element_type=jnp.float32)
        first_ref[part] = first.reshape(hours, few, columns)
        return carry

    lax.fori_loop(0, parts, part_of_first, 0, unroll=8)
    lat = lat_ref[...]

    def hour(t, carry):
        f = first_ref[:, t].reshape(rows, columns).astype(jnp.bfloat16)
        s = jnp.dot(lat, f, preferred_element_type=jnp.float32)
        at = pl.ds(pl.multiple_of(t * STRIDE, 8), rows)
        for k in range(3):
            width = min(LANES, columns - LANES * k)
            second_ref[k, at, :width] = s[:, LANES * k : LANES * k + width]
        return carry

    lax.fori_loop(0, hours, hour, 0, unroll=20)
    row = lax.broadcasted_iota(jnp.int32, (8, LANES), 0)
    lane8 = lax.broadcasted_iota(jnp.int32, (8, LANES), 1)
    lane = lax.broadcasted_iota(jnp.int32, (24, LANES), 1)

    def triple(p, even, odd):
        a, b, c = (
            jnp.concatenate(
                [second_ref[jnp.int32(k), pl.ds(jnp.int32(r * third) + p, 24, STRIDE), :] for k in range(3)], axis=1
            )
            for r in range(3)
        )
        b_up = pltpu.roll(b, 104, 1)
        out_ref[even] = pack(
            [tile(a, 0), tile(a, 1), jnp.where(lane < 104, tile(a, 2), tile(b_up, 0)), tile(b_up, 1), tile(b_up, 2)],
            row,
            lane8,
        )
        b_down = pltpu.roll(b, 204, 1)
        c_up = pltpu.roll(c, 180, 1)
        out_ref[odd] = pack(
            [
                tile(b_down, 0),
                jnp.where(lane < 52, tile(b_down, 1), tile(c_up, 1)),
                tile(c_up, 2),
                tile(c_up, 0),
                tile(c_up, 1),
            ],
            row,
            lane8,
        )

    each = out_ref.shape[0] // COPIES

    def leave(n):
        at = pl.ds(n * each, each)
        return pltpu.make_async_copy(out_ref.at[at], to_ref.at[at], sem.at[n])

    def some(n, carry):
        core, z = n // 4, n % 4

        def four(x_lo, inner):
            for i in range(4):
                x_hi, y = i // 2, i % 2 * 2
                at = n * each + y * 4 + x_hi * 2 + x_lo
                triple(z * 16 + x_lo * 8 + core * 4 + i, at, at + 4)
            return inner

        lax.fori_loop(0, 2, four, 0)
        leave(n).start()
        return carry

    lax.fori_loop(0, COPIES, some, 0)
    for n in range(COPIES):
        leave(n).wait()


def mix(x, lon, lat):
    parts, hours, few, columns = x.shape
    rows = lat.shape[0]
    return pl.pallas_call(
        mix_kernel,
        in_specs=[WHOLE] * 3,
        out_specs=OUTSIDE,
        out_shape=pltpu.HBM((2 * rows // 3, BLOCK, LANES), jnp.bfloat16),
        scratch_shapes=[
            pltpu.VMEM((parts, hours, few, columns), jnp.float32),
            pltpu.VMEM((3, 24 * STRIDE, LANES), jnp.float32),
            pltpu.VMEM((2 * rows // 3, BLOCK, LANES), jnp.bfloat16),
            pltpu.SemaphoreType.DMA((COPIES,)),
        ],
        compiler_params=params(24),
    )(x, lon, lat)


def order_kernel(t_ref, move_ref, out_ref):
    move = move_ref[...]
    total = t_ref.shape[1]
    groups = total // GROUP
    main, tail = 16 * MAIN, 16 * (HOURS - MAIN)
    start = 2 * groups * main
    for z in range(groups):
        w = lax.dot_general(
            move,
            t_ref[:, GROUP * z : GROUP * (z + 1)],
            (((0,), (1,)), ((), ())),
            preferred_element_type=jnp.float32,
        ).astype(jnp.bfloat16)
        for core in range(2):
            at = (core * groups + z) * main
            out_ref[at : at + main, :] = w[main * core : main * (core + 1)]
            at = start + (core * groups + z) * tail
            out_ref[at : at + tail, :] = w[2 * main + tail * core : 2 * main + tail * (core + 1)]


def order_columns(time_factor):
    rows, total = time_factor.shape
    col = jnp.arange(GROUP)
    main, tail = 16 * MAIN, 16 * (HOURS - MAIN)
    late = col >= 2 * main
    core = jnp.where(late, (col - 2 * main) // tail, col // main)
    within = jnp.where(late, (col - 2 * main) % tail, col % main)
    device = jnp.where(late, within % 16, within // MAIN)
    which = jnp.where(late, MAIN + within // 16, within % MAIN)
    y, x_hi, x_lo = device // 4, device // 2 % 2, device % 2
    hour = (x_lo * 2 + core) * 8 * HOURS + (x_hi * 4 + y) * HOURS + which
    move = (jnp.arange(GROUP)[:, None] == hour[None, :]).astype(jnp.bfloat16)
    few = 256
    return pl.pallas_call(
        order_kernel,
        grid=(rows // few,),
        in_specs=[pl.BlockSpec((few, total), lambda i: (i, 0)), pl.BlockSpec((GROUP, GROUP), lambda i: (0, 0))],
        out_specs=pl.BlockSpec((total, few), lambda i: (0, i)),
        out_shape=jax.ShapeDtypeStruct((total, rows), jnp.bfloat16),
        compiler_params=params(16),
    )(time_factor, move)


def unpack(r_ref, gt_ref, tail_ref):
    sources = r_ref.shape[0]
    main = sources * MAIN
    few = BLOCK - 64
    tail_ref[...] = r_ref[:, 64:].astype(jnp.float32).reshape(sources * few, LANES)

    def tails(first):
        parts = []
        for u in range(sources // 16):
            for i in range(HOURS - MAIN):
                parts.append(tail_ref[pl.ds(u * 16 * few + first + i, 16, few), :])
        return jnp.concatenate(parts, axis=0)

    for k in range(4):
        at = slice(LANES * k, LANES * (k + 1))
        gt_ref[at, :main] = r_ref[:, 16 * k : 16 * k + 16].reshape(main, LANES).T
        gt_ref[at, main:] = tails(4 * k).T.astype(jnp.bfloat16)
    at = slice(4 * LANES, TALL)
    last = r_ref[:, 80:88].astype(jnp.float32).reshape(sources * 8, LANES)
    both = jnp.concatenate(
        [last.reshape(sources, 1, 8, LANES), pltpu.roll(last, 96, 1).reshape(sources, 1, 8, LANES)], axis=1
    )
    gt_ref[at, :main] = both.reshape(main, LANES).T[: TALL - 4 * LANES].astype(jnp.bfloat16)
    gt_ref[at, main:] = pltpu.roll(tails(16), 64, 1).T[: TALL - 4 * LANES].astype(jnp.bfloat16)


def time_kernel(r_ref, t_ref, out_ref, gt_ref, tail_ref, held_ref, sem):
    few = out_ref.shape[1]
    step = pl.program_id(0)

    def arrival(n):
        at = pl.ds(pl.multiple_of(n * few, few), few)
        return pltpu.make_async_copy(t_ref.at[:, at], held_ref.at[n], sem.at[n])

    @pl.when(step == 0)
    def _():
        arrival(0).start()
        arrival(1).start()
        unpack(r_ref, gt_ref, tail_ref)

    @pl.when(step + 2 < pl.num_programs(0))
    def _():
        arrival(step + 2).start()

    arrival(step).wait()
    w = jnp.dot(gt_ref[...], held_ref[step], preferred_element_type=jnp.float32)
    out_ref[...] = w[:CELLS].astype(jnp.bfloat16)


def time_product(r, t):
    few = 512
    total, out_rows = t.shape
    return pl.pallas_call(
        time_kernel,
        grid=(out_rows // few,),
        in_specs=[WHOLE, OUTSIDE],
        out_specs=pl.BlockSpec((CELLS, few), lambda i: (0, i)),
        out_shape=jax.ShapeDtypeStruct((CELLS, out_rows), jnp.bfloat16),
        scratch_shapes=[
            pltpu.VMEM((TALL, total), jnp.bfloat16),
            pltpu.VMEM((r.shape[0] * (BLOCK - 64), LANES), jnp.float32),
            pltpu.VMEM((out_rows // few, total, few), jnp.bfloat16),
            pltpu.SemaphoreType.DMA((out_rows // few,)),
        ],
        compiler_params=params(40),
    )(r, t)


def by_thirds(lat_factor):
    rows = lat_factor.shape[0]
    return lat_factor.reshape(rows // 3, 3, rows).transpose(1, 0, 2).reshape(rows, rows)


def on_device(field, time_factor, lat_factor, lon_factor):
    hours, few, columns = field.shape
    parts = lax.axis_size(("x_hi", "y"))
    moved = lax.all_to_all(field, ("x_hi", "y"), split_axis=0, concat_axis=0, tiled=True)
    ordered = order_columns(time_factor)
    lat = by_thirds(lat_factor)
    blocks = mix(moved.reshape(parts, hours // parts, few, columns), lon_factor, lat)
    got = lax.all_to_all(blocks, ("core", "z", "y", "x_hi", "x_lo"), split_axis=0, concat_axis=0, tiled=True)
    return time_product(got, ordered).T


def solution(mesh):
    tm, lat = ("z", "x_lo", "core"), ("x_hi", "y")
    parts = jax.sharding.Mesh(mesh.devices.reshape(4, 2, 2, 2, 4), tm + lat)
    return jax.shard_map(
        on_device,
        mesh=parts,
        in_specs=(P(tm, lat, None), P(), P(), P()),
        out_specs=P(None, tm + lat),
        check_vma=False,
    )
```

```python
import jax
import jax.numpy as jnp
from jax import lax
from jax.experimental import pallas as pl
from jax.experimental.pallas import tpu as pltpu
from jax.sharding import PartitionSpec as P

LANES = 128
CELLS = 540
TALL = 544
HOURS = 20
MAIN = 16
BLOCK = 88
GROUP = 32 * HOURS
STRIDE = 200
COPIES = 8
WHOLE = pl.BlockSpec(memory_space=pltpu.VMEM)
OUTSIDE = pl.BlockSpec(memory_space=pltpu.HBM)


def params(mib):
    return pltpu.CompilerParams(vmem_limit_bytes=mib * 1024 * 1024)


def tile(v, k):
    return v[:, LANES * k : LANES * (k + 1)]


def pack(tiles, row, lane):
    tails = [jnp.where(row < 4, tiles[k][16:], pltpu.roll(tiles[k + 1][16:], 4, 0)) for k in (0, 2)]
    rest = tiles[4]
    last = jnp.where(
        lane < 32,
        rest[:8],
        jnp.where(lane < 64, pltpu.roll(rest[8:16], 32, 1), pltpu.roll(rest[16:], 64, 1)),
    )
    return jnp.concatenate([t[:16] for t in tiles[:4]] + tails + [last], axis=0).astype(jnp.bfloat16)


def mix_kernel(x_ref, lon_ref, lat_ref, to_ref, first_ref, second_ref, out_ref, sem):
    parts, hours, few, columns = x_ref.shape
    rows = parts * few
    third = rows // 3
    lon = lon_ref[...]

    def part_of_first(part, carry):
        x = x_ref[part].astype(jnp.float32).reshape(hours * few, columns).astype(jnp.bfloat16)
        first = jnp.dot(x, lon, preferred_element_type=jnp.float32)
        first_ref[part] = first.reshape(hours, few, columns)
        return carry

    lax.fori_loop(0, parts, part_of_first, 0, unroll=8)
    lat = lat_ref[...]

    def hour(t, carry):
        f = first_ref[:, t].reshape(rows, columns).astype(jnp.bfloat16)
        s = jnp.dot(lat, f, preferred_element_type=jnp.float32)
        at = pl.ds(pl.multiple_of(t * STRIDE, 8), rows)
        for k in range(3):
            width = min(LANES, columns - LANES * k)
            second_ref[k, at, :width] = s[:, LANES * k : LANES * k + width]
        return carry

    lax.fori_loop(0, hours, hour, 0, unroll=20)
    row = lax.broadcasted_iota(jnp.int32, (8, LANES), 0)
    lane8 = lax.broadcasted_iota(jnp.int32, (8, LANES), 1)
    lane = lax.broadcasted_iota(jnp.int32, (24, LANES), 1)

    def triple(p, even, odd):
        a, b, c = (
            jnp.concatenate(
                [second_ref[jnp.int32(k), pl.ds(jnp.int32(r * third) + p, 24, STRIDE), :] for k in range(3)], axis=1
            )
            for r in range(3)
        )
        b_up = pltpu.roll(b, 104, 1)
        out_ref[even] = pack(
            [tile(a, 0), tile(a, 1), jnp.where(lane < 104, tile(a, 2), tile(b_up, 0)), tile(b_up, 1), tile(b_up, 2)],
            row,
            lane8,
        )
        b_down = pltpu.roll(b, 204, 1)
        c_up = pltpu.roll(c, 180, 1)
        out_ref[odd] = pack(
            [
                tile(b_down, 0),
                jnp.where(lane < 52, tile(b_down, 1), tile(c_up, 1)),
                tile(c_up, 2),
                tile(c_up, 0),
                tile(c_up, 1),
            ],
            row,
            lane8,
        )

    each = out_ref.shape[0] // COPIES

    def leave(n):
        at = pl.ds(n * each, each)
        return pltpu.make_async_copy(out_ref.at[at], to_ref.at[at], sem.at[n])

    def some(n, carry):
        core, z = n // 4, n % 4

        def four(x_lo, inner):
            for i in range(4):
                x_hi, y = i // 2, i % 2 * 2
                at = n * each + y * 4 + x_hi * 2 + x_lo
                triple(z * 16 + x_lo * 8 + core * 4 + i, at, at + 4)
            return inner

        lax.fori_loop(0, 2, four, 0)
        leave(n).start()
        return carry

    lax.fori_loop(0, COPIES, some, 0)
    for n in range(COPIES):
        leave(n).wait()


def mix(x, lon, lat):
    parts, hours, few, columns = x.shape
    rows = lat.shape[0]
    return pl.pallas_call(
        mix_kernel,
        in_specs=[WHOLE] * 3,
        out_specs=OUTSIDE,
        out_shape=pltpu.HBM((2 * rows // 3, BLOCK, LANES), jnp.bfloat16),
        scratch_shapes=[
            pltpu.VMEM((parts, hours, few, columns), jnp.float32),
            pltpu.VMEM((3, 24 * STRIDE, LANES), jnp.float32),
            pltpu.VMEM((2 * rows // 3, BLOCK, LANES), jnp.bfloat16),
            pltpu.SemaphoreType.DMA((COPIES,)),
        ],
        compiler_params=params(24),
    )(x, lon, lat)


def order_kernel(t_ref, move_ref, out_ref):
    move = move_ref[...]
    total = t_ref.shape[1]
    groups = total // GROUP
    main, tail = 16 * MAIN, 16 * (HOURS - MAIN)
    start = 2 * groups * main
    for z in range(groups):
        w = lax.dot_general(
            move,
            t_ref[:, GROUP * z : GROUP * (z + 1)],
            (((0,), (1,)), ((), ())),
            preferred_element_type=jnp.float32,
        ).astype(jnp.bfloat16)
        for core in range(2):
            at = (core * groups + z) * main
            out_ref[at : at + main, :] = w[main * core : main * (core + 1)]
            at = start + (core * groups + z) * tail
            out_ref[at : at + tail, :] = w[2 * main + tail * core : 2 * main + tail * (core + 1)]


def order_columns(time_factor):
    rows, total = time_factor.shape
    col = jnp.arange(GROUP)
    main, tail = 16 * MAIN, 16 * (HOURS - MAIN)
    late = col >= 2 * main
    core = jnp.where(late, (col - 2 * main) // tail, col // main)
    within = jnp.where(late, (col - 2 * main) % tail, col % main)
    device = jnp.where(late, within % 16, within // MAIN)
    which = jnp.where(late, MAIN + within // 16, within % MAIN)
    y, x_hi, x_lo = device // 4, device // 2 % 2, device % 2
    hour = (x_lo * 2 + core) * 8 * HOURS + (x_hi * 4 + y) * HOURS + which
    move = (jnp.arange(GROUP)[:, None] == hour[None, :]).astype(jnp.bfloat16)
    few = 256
    return pl.pallas_call(
        order_kernel,
        grid=(rows // few,),
        in_specs=[pl.BlockSpec((few, total), lambda i: (i, 0)), pl.BlockSpec((GROUP, GROUP), lambda i: (0, 0))],
        out_specs=pl.BlockSpec((total, few), lambda i: (0, i)),
        out_shape=jax.ShapeDtypeStruct((total, rows), jnp.bfloat16),
        compiler_params=params(16),
    )(time_factor, move)


def unpack(r_ref, gt_ref, tail_ref):
    sources = r_ref.shape[0]
    main = sources * MAIN
    few = BLOCK - 64
    tail_ref[...] = r_ref[:, 64:].astype(jnp.float32).reshape(sources * few, LANES)

    def tails(first):
        parts = []
        for u in range(sources // 16):
            for i in range(HOURS - MAIN):
                parts.append(tail_ref[pl.ds(u * 16 * few + first + i, 16, few), :])
        return jnp.concatenate(parts, axis=0)

    for k in range(4):
        at = slice(LANES * k, LANES * (k + 1))
        gt_ref[at, :main] = r_ref[:, 16 * k : 16 * k + 16].reshape(main, LANES).T
        gt_ref[at, main:] = tails(4 * k).T.astype(jnp.bfloat16)
    at = slice(4 * LANES, TALL)
    last = r_ref[:, 80:88].astype(jnp.float32).reshape(sources * 8, LANES)
    both = jnp.concatenate(
        [last.reshape(sources, 1, 8, LANES), pltpu.roll(last, 96, 1).reshape(sources, 1, 8, LANES)], axis=1
    )
    gt_ref[at, :main] = both.reshape(main, LANES).T[: TALL - 4 * LANES].astype(jnp.bfloat16)
    gt_ref[at, main:] = pltpu.roll(tails(16), 64, 1).T[: TALL - 4 * LANES].astype(jnp.bfloat16)


def time_kernel(r_ref, t_ref, out_ref, gt_ref, tail_ref, held_ref, sem):
    few = out_ref.shape[1]
    step = pl.program_id(0)

    def arrival(n):
        at = pl.ds(pl.multiple_of(n * few, few), few)
        return pltpu.make_async_copy(t_ref.at[:, at], held_ref.at[n], sem.at[n])

    @pl.when(step == 0)
    def _():
        arrival(0).start()
        arrival(1).start()
        unpack(r_ref, gt_ref, tail_ref)

    @pl.when(step + 2 < pl.num_programs(0))
    def _():
        arrival(step + 2).start()

    arrival(step).wait()
    w = jnp.dot(gt_ref[...], held_ref[step], preferred_element_type=jnp.float32)
    out_ref[...] = w[:CELLS].astype(jnp.bfloat16)


def time_product(r, t):
    few = 512
    total, out_rows = t.shape
    return pl.pallas_call(
        time_kernel,
        grid=(out_rows // few,),
        in_specs=[WHOLE, OUTSIDE],
        out_specs=pl.BlockSpec((CELLS, few), lambda i: (0, i)),
        out_shape=jax.ShapeDtypeStruct((CELLS, out_rows), jnp.bfloat16),
        scratch_shapes=[
            pltpu.VMEM((TALL, total), jnp.bfloat16),
            pltpu.VMEM((r.shape[0] * (BLOCK - 64), LANES), jnp.float32),
            pltpu.VMEM((out_rows // few, total, few), jnp.bfloat16),
            pltpu.SemaphoreType.DMA((out_rows // few,)),
        ],
        compiler_params=params(40),
    )(r, t)


def by_thirds(lat_factor):
    rows = lat_factor.shape[0]
    return lat_factor.reshape(rows // 3, 3, rows).transpose(1, 0, 2).reshape(rows, rows)


def on_device(field, time_factor, lat_factor, lon_factor):
    hours, few, columns = field.shape
    parts = lax.axis_size(("x_hi", "y"))
    moved = lax.all_to_all(field, ("x_hi", "y"), split_axis=0, concat_axis=0, tiled=True)
    ordered = order_columns(time_factor)
    lat = by_thirds(lat_factor)
    moved, ordered = lax.optimization_barrier((moved, ordered))
    blocks = mix(moved.reshape(parts, hours // parts, few, columns), lon_factor, lat)
    got = lax.all_to_all(blocks, ("core", "z", "y", "x_hi", "x_lo"), split_axis=0, concat_axis=0, tiled=True)
    return time_product(got, ordered).T


def solution(mesh):
    tm, lat = ("z", "x_lo", "core"), ("x_hi", "y")
    parts = jax.sharding.Mesh(mesh.devices.reshape(4, 2, 2, 2, 4), tm + lat)
    return jax.shard_map(
        on_device,
        mesh=parts,
        in_specs=(P(tm, lat, None), P(), P(), P()),
        out_specs=P(None, tm + lat),
        check_vma=False,
    )
```

```python
import jax
import jax.numpy as jnp
from jax import lax
from jax.experimental import pallas as pl
from jax.experimental.pallas import tpu as pltpu
from jax.sharding import PartitionSpec as P

LANES = 128
CELLS = 540
TALL = 544
HOURS = 20
MAIN = 16
BLOCK = 88
GROUP = 32 * HOURS
STRIDE = 200
COPIES = 8
WHOLE = pl.BlockSpec(memory_space=pltpu.VMEM)
OUTSIDE = pl.BlockSpec(memory_space=pltpu.HBM)


def params(mib):
    return pltpu.CompilerParams(vmem_limit_bytes=mib * 1024 * 1024)


def tile(v, k):
    return v[:, LANES * k : LANES * (k + 1)]


def pack(tiles, row, lane):
    tails = [jnp.where(row < 4, tiles[k][16:], pltpu.roll(tiles[k + 1][16:], 4, 0)) for k in (0, 2)]
    rest = tiles[4]
    last = jnp.where(
        lane < 32,
        rest[:8],
        jnp.where(lane < 64, pltpu.roll(rest[8:16], 32, 1), pltpu.roll(rest[16:], 64, 1)),
    )
    return jnp.concatenate([t[:16] for t in tiles[:4]] + tails + [last], axis=0).astype(jnp.bfloat16)


def mix_kernel(x_ref, lon_ref, lat_ref, to_ref, first_ref, second_ref, out_ref, sem):
    parts, hours, few, columns = x_ref.shape
    rows = parts * few
    third = rows // 3
    lon = lon_ref[...]

    def part_of_first(part, carry):
        x = x_ref[part].astype(jnp.float32).reshape(hours * few, columns).astype(jnp.bfloat16)
        first = jnp.dot(x, lon, preferred_element_type=jnp.float32)
        first_ref[part] = first.reshape(hours, few, columns)
        return carry

    lax.fori_loop(0, parts, part_of_first, 0, unroll=8)
    lat = lat_ref[...]

    def hour(t, carry):
        f = first_ref[:, t].reshape(rows, columns).astype(jnp.bfloat16)
        s = jnp.dot(lat, f, preferred_element_type=jnp.float32)
        at = pl.ds(pl.multiple_of(t * STRIDE, 8), rows)
        for k in range(3):
            width = min(LANES, columns - LANES * k)
            second_ref[k, at, :width] = s[:, LANES * k : LANES * k + width]
        return carry

    lax.fori_loop(0, hours, hour, 0, unroll=20)
    row = lax.broadcasted_iota(jnp.int32, (8, LANES), 0)
    lane8 = lax.broadcasted_iota(jnp.int32, (8, LANES), 1)
    lane = lax.broadcasted_iota(jnp.int32, (24, LANES), 1)

    def triple(p, even, odd):
        a, b, c = (
            jnp.concatenate(
                [second_ref[jnp.int32(k), pl.ds(jnp.int32(r * third) + p, 24, STRIDE), :] for k in range(3)], axis=1
            )
            for r in range(3)
        )
        b_up = pltpu.roll(b, 104, 1)
        out_ref[even] = pack(
            [tile(a, 0), tile(a, 1), jnp.where(lane < 104, tile(a, 2), tile(b_up, 0)), tile(b_up, 1), tile(b_up, 2)],
            row,
            lane8,
        )
        b_down = pltpu.roll(b, 204, 1)
        c_up = pltpu.roll(c, 180, 1)
        out_ref[odd] = pack(
            [
                tile(b_down, 0),
                jnp.where(lane < 52, tile(b_down, 1), tile(c_up, 1)),
                tile(c_up, 2),
                tile(c_up, 0),
                tile(c_up, 1),
            ],
            row,
            lane8,
        )

    each = out_ref.shape[0] // COPIES

    def leave(n):
        at = pl.ds(n * each, each)
        return pltpu.make_async_copy(out_ref.at[at], to_ref.at[at], sem.at[n])

    def some(n, carry):
        core, z = n // 4, n % 4

        def four(x_lo, inner):
            for i in range(4):
                x_hi, y = i // 2, i % 2 * 2
                at = n * each + y * 4 + x_hi * 2 + x_lo
                triple(z * 16 + x_lo * 8 + core * 4 + i, at, at + 4)
            return inner

        lax.fori_loop(0, 2, four, 0)
        leave(n).start()
        return carry

    lax.fori_loop(0, COPIES, some, 0)
    for n in range(COPIES):
        leave(n).wait()


def mix(x, lon, lat):
    parts, hours, few, columns = x.shape
    rows = lat.shape[0]
    return pl.pallas_call(
        mix_kernel,
        in_specs=[WHOLE] * 3,
        out_specs=OUTSIDE,
        out_shape=pltpu.HBM((2 * rows // 3, BLOCK, LANES), jnp.bfloat16),
        scratch_shapes=[
            pltpu.VMEM((parts, hours, few, columns), jnp.float32),
            pltpu.VMEM((3, 24 * STRIDE, LANES), jnp.float32),
            pltpu.VMEM((2 * rows // 3, BLOCK, LANES), jnp.bfloat16),
            pltpu.SemaphoreType.DMA((COPIES,)),
        ],
        compiler_params=params(24),
    )(x, lon, lat)


def order_kernel(t_ref, move_ref, out_ref):
    move = move_ref[...]
    total = t_ref.shape[1]
    groups = total // GROUP
    main, tail = 16 * MAIN, 16 * (HOURS - MAIN)
    start = 2 * groups * main
    for z in range(groups):
        w = lax.dot_general(
            move,
            t_ref[:, GROUP * z : GROUP * (z + 1)],
            (((0,), (1,)), ((), ())),
            preferred_element_type=jnp.float32,
        ).astype(jnp.bfloat16)
        for core in range(2):
            at = (core * groups + z) * main
            out_ref[at : at + main, :] = w[main * core : main * (core + 1)]
            at = start + (core * groups + z) * tail
            out_ref[at : at + tail, :] = w[2 * main + tail * core : 2 * main + tail * (core + 1)]


def order_columns(time_factor):
    rows, total = time_factor.shape
    col = jnp.arange(GROUP)
    main, tail = 16 * MAIN, 16 * (HOURS - MAIN)
    late = col >= 2 * main
    core = jnp.where(late, (col - 2 * main) // tail, col // main)
    within = jnp.where(late, (col - 2 * main) % tail, col % main)
    device = jnp.where(late, within % 16, within // MAIN)
    which = jnp.where(late, MAIN + within // 16, within % MAIN)
    y, x_hi, x_lo = device // 4, device // 2 % 2, device % 2
    hour = (x_lo * 2 + core) * 8 * HOURS + (x_hi * 4 + y) * HOURS + which
    move = (jnp.arange(GROUP)[:, None] == hour[None, :]).astype(jnp.bfloat16)
    few = 256
    return pl.pallas_call(
        order_kernel,
        grid=(rows // few,),
        in_specs=[pl.BlockSpec((few, total), lambda i: (i, 0)), pl.BlockSpec((GROUP, GROUP), lambda i: (0, 0))],
        out_specs=pl.BlockSpec((total, few), lambda i: (0, i)),
        out_shape=pltpu.HBM((total, rows), jnp.bfloat16),
        compiler_params=params(16),
    )(time_factor, move)


def unpack(r_ref, gt_ref, tail_ref):
    sources = r_ref.shape[0]
    main = sources * MAIN
    few = BLOCK - 64
    tail_ref[...] = r_ref[:, 64:].astype(jnp.float32).reshape(sources * few, LANES)

    def tails(first):
        parts = []
        for u in range(sources // 16):
            for i in range(HOURS - MAIN):
                parts.append(tail_ref[pl.ds(u * 16 * few + first + i, 16, few), :])
        return jnp.concatenate(parts, axis=0)

    for k in range(4):
        at = slice(LANES * k, LANES * (k + 1))
        gt_ref[at, :main] = r_ref[:, 16 * k : 16 * k + 16].reshape(main, LANES).T
        gt_ref[at, main:] = tails(4 * k).T.astype(jnp.bfloat16)
    at = slice(4 * LANES, TALL)
    last = r_ref[:, 80:88].astype(jnp.float32).reshape(sources * 8, LANES)
    both = jnp.concatenate(
        [last.reshape(sources, 1, 8, LANES), pltpu.roll(last, 96, 1).reshape(sources, 1, 8, LANES)], axis=1
    )
    gt_ref[at, :main] = both.reshape(main, LANES).T[: TALL - 4 * LANES].astype(jnp.bfloat16)
    gt_ref[at, main:] = pltpu.roll(tails(16), 64, 1).T[: TALL - 4 * LANES].astype(jnp.bfloat16)


def time_kernel(r_ref, t_ref, out_ref, gt_ref, tail_ref, held_ref, sem):
    few = out_ref.shape[1]
    step = pl.program_id(0)

    def arrival(n):
        at = pl.ds(pl.multiple_of(n * few, few), few)
        return pltpu.make_async_copy(t_ref.at[:, at], held_ref.at[n], sem.at[n])

    @pl.when(step == 0)
    def _():
        arrival(0).start()
        arrival(1).start()
        unpack(r_ref, gt_ref, tail_ref)

    @pl.when(step + 2 < pl.num_programs(0))
    def _():
        arrival(step + 2).start()

    arrival(step).wait()
    w = jnp.dot(gt_ref[...], held_ref[step], preferred_element_type=jnp.float32)
    out_ref[...] = w[:CELLS].astype(jnp.bfloat16)


def time_product(r, t):
    few = 512
    total, out_rows = t.shape
    return pl.pallas_call(
        time_kernel,
        grid=(out_rows // few,),
        in_specs=[WHOLE, OUTSIDE],
        out_specs=pl.BlockSpec((CELLS, few), lambda i: (0, i)),
        out_shape=jax.ShapeDtypeStruct((CELLS, out_rows), jnp.bfloat16),
        scratch_shapes=[
            pltpu.VMEM((TALL, total), jnp.bfloat16),
            pltpu.VMEM((r.shape[0] * (BLOCK - 64), LANES), jnp.float32),
            pltpu.VMEM((out_rows // few, total, few), jnp.bfloat16),
            pltpu.SemaphoreType.DMA((out_rows // few,)),
        ],
        compiler_params=params(40),
    )(r, t)


def by_thirds(lat_factor):
    rows = lat_factor.shape[0]
    return lat_factor.reshape(rows // 3, 3, rows).transpose(1, 0, 2).reshape(rows, rows)


def on_device(field, time_factor, lat_factor, lon_factor):
    hours, few, columns = field.shape
    parts = lax.axis_size(("x_hi", "y"))
    moved = lax.all_to_all(field, ("x_hi", "y"), split_axis=0, concat_axis=0, tiled=True)
    ordered = order_columns(time_factor)
    lat = by_thirds(lat_factor)
    moved, ordered = lax.optimization_barrier((moved, ordered))
    blocks = mix(moved.reshape(parts, hours // parts, few, columns), lon_factor, lat)
    got = lax.all_to_all(blocks, ("core", "z", "y", "x_hi", "x_lo"), split_axis=0, concat_axis=0, tiled=True)
    return time_product(got, ordered).T


def solution(mesh):
    tm, lat = ("z", "x_lo", "core"), ("x_hi", "y")
    parts = jax.sharding.Mesh(mesh.devices.reshape(4, 2, 2, 2, 4), tm + lat)
    return jax.shard_map(
        on_device,
        mesh=parts,
        in_specs=(P(tm, lat, None), P(), P(), P()),
        out_specs=P(None, tm + lat),
        check_vma=False,
    )
```
